32 devices in a mesh: seq: 8 (over z, y), tp: 4 (over x, core).
Axes of the slice: x: 2, y: 2, z: 4, core: 2. Of those that a mesh axis runs over, the one named last changes fastest.
Arguments:
- hidden_in: bfloat16 [1024, 1536], P('seq'), may hold values from -6 to 6
- w_query: bfloat16 [1536, 1536], P(None, 'tp'), may hold values from -0.625 to 0.625
- key_weight: bfloat16 [1536, 512], P(None, 'tp'), may hold values from -0.625 to 0.625
- value_weight: bfloat16 [1536, 512], P(None, 'tp'), may hold values from -0.15625 to 0.15625
- w_out: bfloat16 [1536, 1536], P('tp'), may hold values from -0.4375 to 0.4375
- cached_prefix_keys: bfloat16 [256, 512], P('seq', 'tp'), may hold values from -60000 to 60000
- cached_prefix_values: bfloat16 [256, 512], P('seq', 'tp'), may hold values from -6 to 6
- doc_ids: int32 [8, 128], P('seq'), may hold values from 0 to 3, never falling along the last dimension, each value on 1 to 64 neighbouring positions
- routes: int32 [1024, 8], P(('seq', 'tp')), may hold values from 0 to 31, all different within a row; in each aligned block of 32 rows (0 to 31, 32 to 63, ...) at most 16 rows name the same one
- gate_scores: float32 [1024, 8], P(('seq', 'tp')), may hold values from 0.2 to 1
- expert_in: bfloat16 [32, 1536, 1024], P('seq'), may hold values from -0.15625 to 0.15625
- expert_out: bfloat16 [32, 512, 1536], P('seq'), may hold values from -0.25 to 0.25
Outputs:
- attn_proj: bfloat16 [1024, 1536], P(('seq', 'tp'))
- expert_mix: bfloat16 [1024, 1536], P(('seq', 'tp'))
- layer_out: bfloat16 [1024, 1536], P(('seq', 'tp'))
The draws below stay inside these ranges and needn't reach their ends.
Inputs may be any that keep to these rules, and one draw needn't show every extreme that they name: `routes`: within the rows of one device (aligned blocks of 32 tokens) no expert is picked by more than 16 tokens, a bound that some block reaches; every expert is picked somewhere.
All inputs are finite; a program needn't handle non-finite values.
Results may differ from the reference program's by a relative error of at most 0.028.
Values may be sent and summed in bfloat16 or wider, within the bound.
A program may use at most 64 MiB of HBM per device.

```python
import math
import jax
import jax.numpy as jnp
import numpy as np
from jax import lax

MODEL_WIDTH = 1536
QUERY_HEADS = 24
KEY_VALUE_HEADS = 8
HEAD_WIDTH = 64
FF_E = 512
EXPERTS = 32
TOP = 8
SUFFIX_TOKENS = 128
DOCS_DEV = 4
TOKENS = 1024
PREFIX_TOKENS = 256
MOE_ROWS = 32
CAP = 16
HPARTS = 1
UNITS = 32
FF_S = 512
N_SEQ = 8
N_TP = 4


def draw_cached_prefix_keys(key, part):
    streams = jax.random.split(key, 3)
    column_list = KEY_VALUE_HEADS * HEAD_WIDTH
    entries = jax.random.normal(streams[0], (PREFIX_TOKENS, column_list), jnp.float32)
    row_scale = jnp.exp(jax.random.uniform(streams[1], (PREFIX_TOKENS, 1), jnp.float32, math.log(4.5), math.log(5.5)))
    col_scale = jnp.exp(jax.random.uniform(streams[2], (1, column_list), jnp.float32, math.log(0.5), math.log(2.0)))
    scaled = entries * row_scale * col_scale
    return scaled.astype(jnp.bfloat16)


def shard_levels(key, shape, pieces, low, top_value):
    factor_of, own = 1.0, jax.random.fold_in(key, 6)
    for dim, parts in pieces:
        heights = jnp.exp(jax.random.uniform(jax.random.fold_in(own, dim), (parts,), jnp.float32, low / len(pieces), top_value / len(pieces)))
        factor_of = factor_of * jnp.repeat(heights, shape[dim] // parts).reshape([-1 if axis == dim else 1 for axis in range(len(shape))])
    return factor_of


def length_profile(number_of, total, limit, lean):
    loads = [(1 << 20) // math.isqrt(grade ** lean) + 1 for grade in range(2, number_of + 1)]
    rest, given = total - limit - (number_of - 1), [1] * (number_of - 1)
    while rest > 0:
        candidates = [i for i in range(number_of - 1) if given[i] < limit]
        pool, remaining = sum([loads[i] for i in candidates]), rest
        for i in candidates:
            more = min(limit - given[i], max(1, remaining * loads[i] // pool), rest)
            given[i] = given[i] + more
            rest = rest - more
    return np.array([limit] + given)


def uneven(rng, amount, total, most, skew):
    if amount == 2:
        one = jax.random.randint(rng, (), max(1, total - most), min(most, total - 1) + 1)
        return jnp.stack([one, total - one])
    tallies = jnp.asarray(length_profile(amount, total, most, skew), jnp.int32)
    twos = (amount - 1) // 2
    donor, sink = tallies[1:1 + 2 * twos:2], tallies[2:2 + 2 * twos:2]
    margin = jnp.minimum(donor - 1, most - sink)
    passed = jax.random.randint(jax.random.fold_in(rng, 1), (twos,), 0, 1 << 20) % (margin + 1)
    tallies = tallies.at[1:1 + 2 * twos:2].set(donor - passed).at[2:2 + 2 * twos:2].set(sink + passed)
    return tallies[jax.random.permutation(jax.random.fold_in(rng, 2), amount)]


def shared_out(rng, own, number, rows, count, top, reach, slope):
    sequence = jax.random.permutation(rng, count)
    packed, common = shares(count, rows * top, reach, slope, True), shares(count, rows * top, reach, slope, False)
    places = jnp.arange(count)

    def named(sizes, offset_by):
        used = int((sizes > 0).sum())
        fixed = max(1, used // 4)
        passed = fixed + (places - fixed + offset_by * (used - fixed)) % max(1, count - fixed)
        return jnp.zeros((count,), jnp.int32).at[sequence[jnp.where(places < fixed, places, passed)]].set(jnp.asarray(sizes, jnp.int32))

    sizes = jnp.where(number % 4 == 0, named(packed, number // 4), named(common, number - number // 4 - 1))
    mixed = jax.random.permutation(jax.random.fold_in(own, 3), count)
    donor, sink = mixed[0:count // 2 * 2:2], mixed[1:count // 2 * 2:2]
    slack = jnp.minimum(sizes[donor] - 1, reach - sizes[sink]) // 2
    slack = jnp.where((donor == sequence[0]) | (sink == sequence[0]) | (sizes[sink] == 0), 0, jnp.maximum(slack, 0))
    passed = jax.random.randint(jax.random.fold_in(own, 4), (count // 2,), 0, 1 << 20) % (slack + 1)
    sizes = sizes.at[donor].add(-passed).at[sink].add(passed)
    items = jnp.searchsorted(jnp.cumsum(sizes), jnp.arange(rows * top), side="right").astype(jnp.int32)
    listing = items.reshape(top, rows).T
    listing = listing[jax.random.permutation(jax.random.fold_in(own, 1), rows)]
    offset_by = jax.random.randint(jax.random.fold_in(own, 2), (rows, 1), 0, top)
    return jnp.take_along_axis(listing, (jnp.arange(top)[None, :] + offset_by) % top, axis=1)


def shares(count, total, most, skew, full):
    loads = [(1 << 20) // math.isqrt(grade ** skew) + 1 for grade in range(1, count + 1)]
    largest = most if full else min(most, max(-(-total // count), total * loads[0] // sum(loads)))
    least = 1 if total - largest >= count - 1 else 0
    holding, rest = [largest] + [least] * (count - 1), total - largest - least * (count - 1)
    while rest > 0:
        free = [i for i in range(1, count) if holding[i] < largest] or [i for i in range(1, count) if holding[i] < most]
        pool, budget = sum([loads[i] for i in free]), rest
        for i in free:
            more = min(most - holding[i], max(1, budget * loads[i] // pool), rest)
            holding[i] = holding[i] + more
            rest = rest - more
    return np.array(holding)


def normal_values(rng, dims, width, most, cuts=(), kind=jnp.bfloat16):
    loudness = shard_levels(rng, dims, cuts, -0.22, 0.18) if cuts else 1.0
    drawn = jax.random.normal(rng, dims, jnp.float32) * width * loudness
    return jnp.minimum(jnp.maximum(drawn, -most), most).astype(kind)


def setup_inputs(seed: int = 0) -> dict:
    keys = jax.random.split(jax.random.key(seed), 13)
    hidden_in = normal_values(keys[0], (TOKENS, MODEL_WIDTH), 1.0, 6.0, ((0, 8),))
    w_query = normal_values(keys[1], (MODEL_WIDTH, QUERY_HEADS * HEAD_WIDTH), (MODEL_WIDTH // 16) ** -0.5, 0.625, ((1, 4),))
    key_weight = normal_values(keys[2], (MODEL_WIDTH, KEY_VALUE_HEADS * HEAD_WIDTH), (MODEL_WIDTH // 16) ** -0.5, 0.625, ((1, 4),))
    value_weight = normal_values(keys[3], (MODEL_WIDTH, KEY_VALUE_HEADS * HEAD_WIDTH), MODEL_WIDTH ** -0.5, 0.15625, ((1, 4),))
    w_out = normal_values(keys[4], (QUERY_HEADS * HEAD_WIDTH, MODEL_WIDTH), (QUERY_HEADS * HEAD_WIDTH // 8) ** -0.5, 0.4375, ((0, 4),))
    cached_prefix_keys = draw_cached_prefix_keys(jax.random.fold_in(keys[12], 71), 0)
    cached_prefix_values = normal_values(keys[6], (PREFIX_TOKENS, KEY_VALUE_HEADS * HEAD_WIDTH), 1.0, 6.0, ((0, 8), (1, 4)))
    doc_ids = jax.vmap(lambda own: jnp.searchsorted(jnp.cumsum(uneven(own, DOCS_DEV, SUFFIX_TOKENS, SUFFIX_TOKENS // 2, 2)), jnp.arange(SUFFIX_TOKENS), side="right"))(jax.random.split(keys[7], N_SEQ)).reshape((N_SEQ, SUFFIX_TOKENS)).astype(jnp.int32)
    routes_keys = jax.random.split(jax.random.fold_in(keys[8], 1), TOKENS // MOE_ROWS)
    routes_turns = jax.random.permutation(jax.random.fold_in(keys[8], 3), TOKENS // MOE_ROWS)
    routes = jax.vmap(lambda own, number: shared_out(jax.random.fold_in(keys[8], 2), own, number, MOE_ROWS, EXPERTS, TOP, CAP, 2))(routes_keys, routes_turns).reshape((TOKENS, TOP))
    gate_scores = jnp.clip(0.2 + 0.8 * jax.random.uniform(keys[9], (TOKENS, TOP), jnp.float32) ** shard_levels(keys[9], (TOKENS, TOP), ((0, 32),), -0.2, 0.2), 0.2, 1.0)
    expert_in = normal_values(keys[10], (UNITS, MODEL_WIDTH, 2 * FF_S), MODEL_WIDTH ** -0.5, 0.15625, ((0, 8),))
    expert_out = normal_values(keys[11], (UNITS, FF_S, MODEL_WIDTH), FF_E ** -0.5, 0.25, ((0, 8),))
    return {"hidden_in": hidden_in, "w_query": w_query, "key_weight": key_weight, "value_weight": value_weight, "w_out": w_out, "cached_prefix_keys": cached_prefix_keys, "cached_prefix_values": cached_prefix_values, "doc_ids": doc_ids, "routes": routes, "gate_scores": gate_scores, "expert_in": expert_in, "expert_out": expert_out}


EPSILON = 1e-06
RESIDUAL = 0.22

def normalize(values):
    values = values.astype(jnp.float32)
    return values * lax.rsqrt(lax.optimization_barrier(jnp.mean(values * values, axis=-1, keepdims=True)) + EPSILON)

def rotary_apply(values, token_positions):
    half_size = values.shape[-1] // 2
    frequency = jnp.exp(-jnp.log(10000.0) * jnp.arange(half_size, dtype=jnp.float32) * 2.0 / values.shape[-1])
    angles = token_positions[:, None] * frequency[None, :]
    cosine = jnp.cos(angles)[:, None, :]
    sine_part = jnp.sin(angles)[:, None, :]
    first_half = values[..., :half_size]
    second = values[..., half_size:]
    return jnp.concatenate([first_half * cosine - second * sine_part, second * cosine + first_half * sine_part], axis=-1)

def rounded_value(values):
    return lax.optimization_barrier(values.astype(jnp.bfloat16)).astype(jnp.float32)

def reference(hidden_in, w_query, key_weight, value_weight, w_out, cached_prefix_keys, cached_prefix_values, doc_ids, routes, gate_scores, expert_in, expert_out):
    group_width = QUERY_HEADS // KEY_VALUE_HEADS
    earlier_keys = cached_prefix_keys.astype(jnp.float32).reshape(PREFIX_TOKENS, KEY_VALUE_HEADS, HEAD_WIDTH)
    earlier_values = cached_prefix_values.astype(jnp.float32).reshape(PREFIX_TOKENS, KEY_VALUE_HEADS, HEAD_WIDTH)

    def attend(block_args):
        block_rows, doc_row = block_args
        row_index = jnp.arange(SUFFIX_TOKENS, dtype=jnp.int32)
        same_doc = doc_row[:, None] == doc_row[None, :]
        doc_start = lax.optimization_barrier(jnp.min(jnp.where(same_doc, row_index[None, :], SUFFIX_TOKENS), axis=1))
        token_positions = (PREFIX_TOKENS + row_index - doc_start).astype(jnp.float32)
        normed_input = normalize(block_rows).astype(jnp.bfloat16)
        query_rows_all = jnp.dot(normed_input, w_query, preferred_element_type=jnp.float32).reshape(SUFFIX_TOKENS, QUERY_HEADS, HEAD_WIDTH)
        query_rows_all = rounded_value(rotary_apply(query_rows_all, token_positions)).reshape(SUFFIX_TOKENS, KEY_VALUE_HEADS, group_width, HEAD_WIDTH)
        fresh_key = jnp.dot(normed_input, key_weight, preferred_element_type=jnp.float32).reshape(SUFFIX_TOKENS, KEY_VALUE_HEADS, HEAD_WIDTH)
        fresh_key = rounded_value(rotary_apply(fresh_key, token_positions))
        fresh_value = rounded_value(jnp.dot(normed_input, value_weight, preferred_element_type=jnp.float32)).reshape(SUFFIX_TOKENS, KEY_VALUE_HEADS, HEAD_WIDTH)
        scores_pre = jnp.einsum('tkgd,pkd->tkgp', query_rows_all, earlier_keys) / HEAD_WIDTH
        scores_own = jnp.einsum('tkgd,skd->tkgs', query_rows_all, fresh_key) / HEAD_WIDTH
        visible = same_doc & (row_index[None, :] <= row_index[:, None])
        scores_own = jnp.where(visible[:, None, None, :], scores_own, -jnp.inf)
        row_top = jnp.maximum(lax.optimization_barrier(jnp.max(scores_pre, axis=-1)), lax.optimization_barrier(jnp.max(scores_own, axis=-1)))
        weights_pre = jnp.exp(scores_pre - row_top[..., None])
        weights_own = jnp.exp(scores_own - row_top[..., None])
        denominator = lax.optimization_barrier(jnp.sum(weights_pre, axis=-1)) + lax.optimization_barrier(jnp.sum(weights_own, axis=-1))
        numerator = jnp.einsum('tkgp,pkd->tkgd', rounded_value(weights_pre), earlier_values)
        numerator = numerator + jnp.einsum('tkgs,skd->tkgd', rounded_value(weights_own), fresh_value)
        return (numerator / denominator[..., None]).astype(jnp.bfloat16).reshape(SUFFIX_TOKENS, QUERY_HEADS * HEAD_WIDTH)
    attended = lax.map(attend, (hidden_in.reshape(N_SEQ, SUFFIX_TOKENS, MODEL_WIDTH), doc_ids)).reshape(TOKENS, QUERY_HEADS * HEAD_WIDTH)
    attn_sum = jnp.dot(attended, w_out, preferred_element_type=jnp.float32)
    residual = hidden_in.astype(jnp.float32) + RESIDUAL * attn_sum
    routed = normalize(residual).astype(jnp.bfloat16)
    slot_limit = N_SEQ * N_TP * CAP
    block_size = math.gcd(512, slot_limit)
    slot_index = jnp.arange(slot_limit, dtype=jnp.int32)

    def expert_step(expert, total):
        hit_mask = routes == expert
        weight = lax.optimization_barrier(jnp.sum(jnp.where(hit_mask, gate_scores, 0.0), axis=1))
        chosen = jnp.any(hit_mask, axis=1)
        chosen_count = jnp.sum(chosen.astype(jnp.int32)).astype(jnp.int32)
        slots = jnp.nonzero(chosen, size=slot_limit, fill_value=0)[0].astype(jnp.int32)
        slot_weight = jnp.where(slot_index < chosen_count, weight[slots], 0.0)
        first_unit = (expert * HPARTS).astype(jnp.int32)
        weight_in = lax.dynamic_slice_in_dim(expert_in, first_unit, HPARTS, 0).astype(jnp.float32)
        weight_back = lax.dynamic_slice_in_dim(expert_out, first_unit, HPARTS, 0).astype(jnp.float32)

        def block_step(step, running):
            begin = (step * block_size).astype(jnp.int32)
            span = lax.dynamic_slice_in_dim(slots, begin, block_size, 0)
            span_weight = lax.dynamic_slice_in_dim(slot_weight, begin, block_size, 0)
            span_rows = routed[span].astype(jnp.float32)
            gate_up = jnp.einsum('rd,pdf->prf', span_rows, weight_in)
            activated = rounded_value(jax.nn.silu(gate_up[..., :FF_S]) * gate_up[..., FF_S:])
            partial_value = rounded_value(jnp.einsum('prf,pfd->prd', activated, weight_back))
            summed = lax.optimization_barrier(jnp.sum(partial_value, axis=0))
            return running.at[span].add(span_weight[:, None] * summed)
        trip_count = (chosen_count + block_size - 1) // block_size
        return lax.fori_loop(0, trip_count, block_step, total)
    expert_sum = lax.fori_loop(0, EXPERTS, expert_step, jnp.zeros((TOKENS, MODEL_WIDTH), jnp.float32))
    layer_out = (residual + RESIDUAL * expert_sum).astype(jnp.bfloat16)
    return (attn_sum.astype(jnp.bfloat16), expert_sum.astype(jnp.bfloat16), layer_out)
```

```python
import jax
import jax.numpy as jnp
from jax import lax
from jax.sharding import PartitionSpec as P

HEAD_WIDTH = 64
EXPERTS = 32


EPSILON = 1e-06
RESIDUAL = 0.22


def normalize(values):
    values = values.astype(jnp.float32)
    return values * lax.rsqrt(jnp.mean(values * values, axis=-1, keepdims=True) + EPSILON)


def rotary_apply(values, token_positions):
    half_size = values.shape[-1] // 2
    frequency = jnp.exp(
        -jnp.log(10000.0) * jnp.arange(half_size, dtype=jnp.float32) * 2.0 / values.shape[-1]
    )
    angles = token_positions[:, None] * frequency[None, :]
    cosine = jnp.cos(angles)[:, None, :]
    sine_part = jnp.sin(angles)[:, None, :]
    first_half = values[..., :half_size]
    second = values[..., half_size:]
    return jnp.concatenate(
        [first_half * cosine - second * sine_part, second * cosine + first_half * sine_part],
        axis=-1,
    )


def body(
    hidden_in,
    w_query,
    key_weight,
    value_weight,
    w_out,
    cached_prefix_keys,
    cached_prefix_values,
    doc_ids,
    routes,
    gate_scores,
    expert_in,
    expert_out,
):
    rows_dev = hidden_in.shape[0]
    column_list = hidden_in.shape[1]
    head_size = HEAD_WIDTH
    kv_local = key_weight.shape[1] // head_size
    group_width = w_query.shape[1] // head_size // kv_local
    seq_count = lax.axis_size("seq")
    prefix_len = cached_prefix_keys.shape[0] * seq_count
    doc_row = doc_ids[0]
    row_index = jnp.arange(rows_dev, dtype=jnp.int32)
    same_doc = doc_row[:, None] == doc_row[None, :]
    doc_start = jnp.min(jnp.where(same_doc, row_index[None, :], rows_dev), axis=1)
    token_positions = (prefix_len + row_index - doc_start).astype(jnp.float32)
    normed_input = normalize(hidden_in).astype(jnp.bfloat16)
    query_rows_all = jnp.dot(normed_input, w_query, preferred_element_type=jnp.float32).reshape(
        rows_dev, kv_local * group_width, head_size
    )
    query_rows_all = (
        rotary_apply(query_rows_all, token_positions)
        .astype(jnp.bfloat16)
        .reshape(rows_dev, kv_local, group_width, head_size)
    )
    fresh_key = jnp.dot(normed_input, key_weight, preferred_element_type=jnp.float32).reshape(
        rows_dev, kv_local, head_size
    )
    fresh_key = rotary_apply(fresh_key, token_positions).astype(jnp.bfloat16)
    fresh_value = (
        jnp.dot(normed_input, value_weight, preferred_element_type=jnp.float32)
        .astype(jnp.bfloat16)
        .reshape(rows_dev, kv_local, head_size)
    )
    own_scores = (
        jnp.einsum("tkgd,skd->tkgs", query_rows_all, fresh_key, preferred_element_type=jnp.float32)
        / head_size
    )
    visible = same_doc & (row_index[None, :] <= row_index[:, None])
    own_scores = jnp.where(visible[:, None, None, :], own_scores, -jnp.inf)
    row_top = jnp.max(own_scores, axis=-1)
    weights = jnp.exp(own_scores - row_top[..., None])
    denominator = jnp.sum(weights, axis=-1)
    numerator = jnp.einsum(
        "tkgs,skd->tkgd",
        weights.astype(jnp.bfloat16),
        fresh_value,
        preferred_element_type=jnp.float32,
    )
    running = (row_top, denominator, numerator)
    whole_keys, whole_values = (
        lax.all_gather(cached_prefix_keys, "seq", axis=0, tiled=True),
        lax.all_gather(cached_prefix_values, "seq", axis=0, tiled=True),
    )
    top_old, denom_old, numer_old = running
    key_rows = whole_keys.reshape(-1, kv_local, head_size)
    value_rows = whole_values.reshape(-1, kv_local, head_size)
    scores = (
        jnp.einsum("tkgd,pkd->tkgp", query_rows_all, key_rows, preferred_element_type=jnp.float32)
        / head_size
    )
    top_new = jnp.maximum(top_old, jnp.max(scores, axis=-1))
    shrink = jnp.exp(top_old - top_new)
    part_weights = jnp.exp(scores - top_new[..., None])
    denom_new = denom_old * shrink + jnp.sum(part_weights, axis=-1)
    numer_new = numer_old * shrink[..., None] + jnp.einsum(
        "tkgp,pkd->tkgd",
        part_weights.astype(jnp.bfloat16),
        value_rows,
        preferred_element_type=jnp.float32,
    )
    running = (top_new, denom_new, numer_new)
    attended = (
        (running[2] / running[1][..., None])
        .astype(jnp.bfloat16)
        .reshape(rows_dev, kv_local * group_width * head_size)
    )
    moe_rows = routes.shape[0]
    row_start = lax.axis_index("tp") * moe_rows
    summed_all = lax.psum(jnp.dot(attended, w_out, preferred_element_type=jnp.float32), "tp")
    attn_sum = lax.dynamic_slice_in_dim(summed_all, row_start, moe_rows, 0)
    residual = (
        lax.dynamic_slice_in_dim(hidden_in, row_start, moe_rows, 0).astype(jnp.float32)
        + RESIDUAL * attn_sum
    )
    routed = normalize(residual).astype(jnp.bfloat16)
    experts = EXPERTS
    units_dev = expert_in.shape[0]
    hparts = units_dev * seq_count // experts
    capacity = moe_rows // 2
    ff_part = expert_out.shape[1]
    onehot = (routes[:, :, None] == jnp.arange(experts, dtype=jnp.int32)[None, None, :]).astype(
        jnp.int32
    )
    per_row = jnp.sum(onehot, axis=1)
    earlier = (jnp.arange(moe_rows)[None, :] < jnp.arange(moe_rows)[:, None]).astype(jnp.bfloat16)
    before = jnp.dot(
        earlier, per_row.astype(jnp.bfloat16), preferred_element_type=jnp.float32
    ).astype(jnp.int32)
    rank_in = jnp.sum(onehot * before[:, None, :], axis=2)
    slot_of = routes * capacity + rank_in
    slot_ids = jnp.arange(experts * capacity, dtype=jnp.int32)
    pick_hit = slot_of[:, :, None] == slot_ids[None, None, :]
    selector = jnp.any(pick_hit, axis=1).T.astype(jnp.bfloat16)
    combiner = jnp.sum(jnp.where(pick_hit, gate_scores[:, :, None], 0.0), axis=1)
    gathered = jnp.dot(selector, routed, preferred_element_type=jnp.float32).astype(jnp.bfloat16)
    outgoing = jnp.broadcast_to(
        gathered.reshape(experts, 1, capacity, column_list),
        (experts, hparts, capacity, column_list),
    )
    outgoing = outgoing.reshape(seq_count, units_dev, capacity, column_list)
    gate_up = jnp.einsum(
        "sucd,udf->sucf",
        lax.all_to_all(outgoing, "seq", split_axis=0, concat_axis=0, tiled=True),
        expert_in,
        preferred_element_type=jnp.float32,
    )
    activated = (jax.nn.silu(gate_up[..., :ff_part]) * gate_up[..., ff_part:]).astype(jnp.bfloat16)
    partial_value = jnp.einsum(
        "sucf,ufd->sucd", activated, expert_out, preferred_element_type=jnp.float32
    ).astype(jnp.bfloat16)
    returned = lax.all_to_all(partial_value, "seq", split_axis=0, concat_axis=0, tiled=True)
    part_sum = jnp.sum(
        returned.reshape(experts, hparts, capacity, column_list).astype(jnp.float32), axis=1
    )
    part_sum = part_sum.reshape(experts * capacity, column_list)
    expert_sum = jnp.dot(
        combiner, part_sum, precision=lax.Precision.HIGHEST, preferred_element_type=jnp.float32
    )
    layer_out = (residual + RESIDUAL * expert_sum).astype(jnp.bfloat16)
    return (attn_sum.astype(jnp.bfloat16), expert_sum.astype(jnp.bfloat16), layer_out)


def solution(mesh):
    in_specs = (
        P("seq", None),
        P(None, "tp"),
        P(None, "tp"),
        P(None, "tp"),
        P("tp", None),
        P("seq", "tp"),
        P("seq", "tp"),
        P("seq", None),
        P(("seq", "tp"), None),
        P(("seq", "tp"), None),
        P("seq", None, None),
        P("seq", None, None),
    )
    out_specs = (P(("seq", "tp"), None), P(("seq", "tp"), None), P(("seq", "tp"), None))
    return jax.shard_map(body, mesh=mesh, in_specs=in_specs, out_specs=out_specs, check_vma=False)
```

```python
import functools

import jax
import jax.numpy as jnp
from jax import lax
from jax.experimental import pallas as pl
from jax.experimental.pallas import tpu as pltpu
from jax.sharding import PartitionSpec as P

HEAD_WIDTH = 64
EXPERTS = 32
EPSILON = 1e-06
RESIDUAL = 0.22
MESH = pl.DeviceIdType.MESH
F32 = jnp.float32
BF16 = jnp.bfloat16


def normalize(values):
    values = values.astype(F32)
    return values * lax.rsqrt(jnp.mean(values * values, axis=-1, keepdims=True) + EPSILON)


def rotary_apply(values, token_positions):
    half_size = values.shape[-1] // 2
    frequency = jnp.exp(
        -jnp.log(10000.0) * jnp.arange(half_size, dtype=F32) * 2.0 / values.shape[-1]
    )
    angles = token_positions[:, None] * frequency[None, :]
    cosine = jnp.cos(angles)[:, None, :]
    sine_part = jnp.sin(angles)[:, None, :]
    first_half = values[..., :half_size]
    second = values[..., half_size:]
    return jnp.concatenate(
        [first_half * cosine - second * sine_part, second * cosine + first_half * sine_part],
        axis=-1,
    )


def each(start, stop, fn):
    if stop - start <= 8:
        for i in range(start, stop):
            fn(i)
    else:

        @pl.loop(start, stop)
        def _(i):
            fn(i)


def peers(n):
    half = n // 2
    me = lax.axis_index("seq")
    high, low = me // 2, lax.rem(me, 2)

    def ahead(side, step):
        place = low if side == 0 else 1 - low
        return {"seq": lax.rem(high + step, half) * 2 + place}

    def behind(side, step):
        place = low if side == 0 else 1 - low
        return {"seq": lax.rem(high + half - step, half) * 2 + place}

    return half, ahead, behind


def gather_kernel(n, kv_ref, gate_ref, kv_all, gate_all, send, recv, local):
    half, ahead, _ = peers(n)
    own_a = pltpu.make_async_copy(kv_ref, kv_all.at[0, 0], local.at[0])
    own_b = pltpu.make_async_copy(gate_ref, gate_all.at[0, 0], local.at[1])
    own_a.start()
    own_b.start()
    barrier = pltpu.get_barrier_semaphore()

    def greet(side, step):
        pl.semaphore_signal(barrier, inc=1, device_id=ahead(side, step), device_id_type=MESH)

    each(1, half, lambda step: greet(0, step))
    each(0, half, lambda step: greet(1, step))
    pl.semaphore_wait(barrier, n - 1)

    def copies(side, step):
        return [
            pltpu.make_async_remote_copy(
                src_ref=src,
                dst_ref=dst.at[side, step],
                send_sem=send.at[kind, side, step],
                recv_sem=recv.at[kind, side, step],
                device_id=ahead(side, step),
                device_id_type=MESH,
            )
            for kind, (src, dst) in enumerate(((kv_ref, kv_all), (gate_ref, gate_all)))
        ]

    def start(side, step):
        for c in copies(side, step):
            c.start()

    def finish(side, step):
        for c in copies(side, step):
            c.wait()

    each(1, half, lambda step: start(0, step))
    each(0, half, lambda step: start(1, step))
    each(1, half, lambda step: finish(0, step))
    each(0, half, lambda step: finish(1, step))
    own_a.wait()
    own_b.wait()


def gather(n, kv, gates):
    half = n // 2
    vmem = pl.BlockSpec(memory_space=pltpu.VMEM)
    return pl.pallas_call(
        functools.partial(gather_kernel, n),
        out_shape=(
            jax.ShapeDtypeStruct((2, half) + kv.shape, kv.dtype),
            jax.ShapeDtypeStruct((2, half) + gates.shape, gates.dtype),
        ),
        in_specs=[vmem, vmem],
        out_specs=(vmem, vmem),
        scratch_shapes=[
            pltpu.SemaphoreType.DMA((2, 2, half)),
            pltpu.SemaphoreType.DMA((2, 2, half)),
            pltpu.SemaphoreType.DMA((2,)),
        ],
        compiler_params=pltpu.CompilerParams(
            collective_id=0, has_side_effects=True, vmem_limit_bytes=32 << 20
        ),
    )(kv, gates)


def tail_kernel(
    n, n_tp, hparts,
    attended, w_out, hidden, gate_all, in_hbm, out_hbm,
    proj_ref, mix_ref, layer_ref,
    w_in, w_back, sums, outbox, inbox, tok, part, acc, cross, cross_in, home, home_in,
    w_sem, tp_send, tp_recv, tok_send, tok_recv, x_send, x_recv, h_send, h_recv,
):
    half, ahead, behind = peers(n)
    units, ff = out_hbm.shape[0], out_hbm.shape[1]
    rows, width = proj_ref.shape
    me_tp = lax.axis_index("tp")
    chunk = min(4, half)

    def fetch(u):
        return (
            pltpu.make_async_copy(in_hbm.at[u], w_in.at[u], w_sem.at[0, u]),
            pltpu.make_async_copy(out_hbm.at[u], w_back.at[u], w_sem.at[1, u]),
        )

    barrier = pltpu.get_barrier_semaphore()

    def greet(where):
        pl.semaphore_signal(barrier, inc=1, device_id=where, device_id_type=MESH)

    def tp_peer(t):
        return lax.rem(me_tp + t, n_tp)

    each(1, n_tp, lambda t: greet({"tp": tp_peer(t)}))
    each(1, half, lambda d: greet(ahead(0, d)))
    greet(ahead(1, 0))
    for u in range(units):
        for c in fetch(u):
            c.start()
    whole = jnp.dot(attended[...], w_out[...], preferred_element_type=F32)
    sums[...] = whole
    outbox[...] = whole.astype(BF16)
    pl.semaphore_wait(barrier, n_tp - 1 + half)

    def tp_copy(t):
        return pltpu.make_async_remote_copy(
            src_ref=outbox.at[pl.ds(pl.multiple_of(tp_peer(t) * rows, rows), rows)],
            dst_ref=inbox.at[t],
            send_sem=tp_send.at[t],
            recv_sem=tp_recv.at[t],
            device_id={"tp": tp_peer(t)},
            device_id_type=MESH,
        )

    each(1, n_tp, lambda t: tp_copy(t).start())
    mine = pl.ds(pl.multiple_of(me_tp * rows, rows), rows)
    attn_sum = sums[mine, :]
    for t in range(1, n_tp):
        tp_copy(t).wait_recv()
        attn_sum = attn_sum + inbox[t].astype(F32)
    residual = hidden[mine, :].astype(F32) + RESIDUAL * attn_sum
    proj_ref[...] = attn_sum.astype(BF16)
    tok[0, 0] = normalize(residual).astype(BF16)

    def tok_copy(d):
        return pltpu.make_async_remote_copy(
            src_ref=tok.at[0, 0],
            dst_ref=tok.at[0, d],
            send_sem=tok_send.at[0, d],
            recv_sem=tok_recv.at[0, d],
            device_id=ahead(0, d),
            device_id_type=MESH,
        )

    def tok_cross(d):
        return pltpu.make_async_remote_copy(
            src_ref=tok.at[0, d],
            dst_ref=tok.at[1, d],
            send_sem=tok_send.at[1, d],
            recv_sem=tok_recv.at[1, d],
            device_id=ahead(1, 0),
            device_id_type=MESH,
        )

    def relay(d):
        tok_copy(d).wait_recv()
        tok_cross(d).start()

    each(1, half, lambda d: tok_copy(d).start())
    tok_cross(0).start()
    for u in range(units):
        for c in fetch(u):
            c.wait()
    each(1, half, relay)

    first_unit = lax.axis_index("seq") * units

    def experts(side, begin):
        tokens = tok[side, pl.ds(begin, chunk)].reshape(chunk * rows, width)
        gates = gate_all[side, pl.ds(begin, chunk)].reshape(chunk * rows, gate_all.shape[-1])
        lanes = lax.broadcasted_iota(jnp.int32, gates.shape, 1)
        acc[...] = jnp.zeros(acc.shape, F32)

        @pl.loop(0, units)
        def _(u):
            expert = (first_unit + u) // hparts
            weight = jnp.sum(jnp.where(lanes == expert, gates, 0.0), axis=1, keepdims=True)
            gate_up = jnp.dot(tokens, w_in[u], preferred_element_type=F32)
            active = (jax.nn.silu(gate_up[:, :ff]) * gate_up[:, ff:]).astype(BF16)
            back = jnp.dot(active, w_back[u], preferred_element_type=F32).astype(BF16)
            acc[...] += weight * back.astype(F32)

        total = acc[...].reshape(chunk, rows, width)
        if side == 0:
            part[pl.ds(begin, chunk)] = total
        else:
            cross[pl.ds(begin, chunk)] = total.astype(BF16)

    each(0, half // chunk, lambda c: experts(0, c * chunk))

    def cross_copy(d):
        return pltpu.make_async_remote_copy(
            src_ref=cross.at[d],
            dst_ref=cross_in.at[d],
            send_sem=x_send.at[d],
            recv_sem=x_recv.at[d],
            device_id=ahead(1, 0),
            device_id_type=MESH,
        )

    def send_cross(d):
        cross_copy(d).start()

    each(0, half, lambda d: tok_cross(d).wait_recv())
    each(0, half // chunk, lambda c: experts(1, c * chunk))
    each(1, half, send_cross)
    send_cross(0)

    def home_copy(d):
        return pltpu.make_async_remote_copy(
            src_ref=home.at[d],
            dst_ref=home_in.at[d],
            send_sem=h_send.at[d],
            recv_sem=h_recv.at[d],
            device_id=behind(0, d),
            device_id_type=MESH,
        )

    def send_home(d):
        cross_copy(d).wait_recv()
        home[d] = (part[d] + cross_in[d].astype(F32)).astype(BF16)
        home_copy(d).start()

    each(1, half, send_home)
    cross_copy(0).wait_recv()
    part[0] += cross_in[0].astype(F32)

    def collect(d):
        home_copy(d).wait_recv()
        part[0] += home_in[d].astype(F32)

    each(1, half, collect)
    expert_sum = part[0]
    mix_ref[...] = expert_sum.astype(BF16)
    layer_ref[...] = (residual + RESIDUAL * expert_sum).astype(BF16)

    each(1, n_tp, lambda t: tp_copy(t).wait_send())
    each(1, half, lambda d: tok_copy(d).wait_send())
    each(0, half, lambda d: tok_cross(d).wait_send())
    each(0, half, lambda d: cross_copy(d).wait_send())
    each(1, half, lambda d: home_copy(d).wait_send())


def tail(n, n_tp, attended, w_out, hidden, gate_all, expert_in, expert_out):
    half = n // 2
    block, width = hidden.shape
    rows = block // n_tp
    units, ff = expert_out.shape[:2]
    hparts = units * n // EXPERTS
    vmem = pl.BlockSpec(memory_space=pltpu.VMEM)
    hbm = pl.BlockSpec(memory_space=pl.ANY)
    out = jax.ShapeDtypeStruct((rows, width), BF16)
    dma = pltpu.SemaphoreType.DMA
    return pl.pallas_call(
        functools.partial(tail_kernel, n, n_tp, hparts),
        out_shape=(out, out, out),
        in_specs=[vmem, vmem, vmem, vmem, hbm, hbm],
        out_specs=(vmem, vmem, vmem),
        scratch_shapes=[
            pltpu.VMEM(expert_in.shape, BF16),
            pltpu.VMEM(expert_out.shape, BF16),
            pltpu.VMEM((block, width), F32),
            pltpu.VMEM((block, width), BF16),
            pltpu.VMEM((n_tp, rows, width), BF16),
            pltpu.VMEM((2, half, rows, width), BF16),
            pltpu.VMEM((half, rows, width), F32),
            pltpu.VMEM((min(4, half) * rows, width), F32),
            pltpu.VMEM((half, rows, width), BF16),
            pltpu.VMEM((half, rows, width), BF16),
            pltpu.VMEM((half, rows, width), BF16),
            pltpu.VMEM((half, rows, width), BF16),
            dma((2, units)),
            dma((n_tp,)),
            dma((n_tp,)),
            dma((2, half)),
            dma((2, half)),
            dma((half,)),
            dma((half,)),
            dma((half,)),
            dma((half,)),
        ],
        compiler_params=pltpu.CompilerParams(
            collective_id=1,
            has_side_effects=True,
            vmem_limit_bytes=(44 << 20) if half <= 8 else (63 << 20),
        ),
    )(attended, w_out, hidden, gate_all, expert_in, expert_out)


def body(
    hidden_in,
    w_query,
    key_weight,
    value_weight,
    w_out,
    cached_prefix_keys,
    cached_prefix_values,
    doc_ids,
    routes,
    gate_scores,
    expert_in,
    expert_out,
):
    rows_dev = hidden_in.shape[0]
    head_size = HEAD_WIDTH
    kv_width = key_weight.shape[1]
    kv_local = kv_width // head_size
    group_width = w_query.shape[1] // head_size // kv_local
    n, n_tp = lax.axis_size("seq"), lax.axis_size("tp")
    prefix_len = cached_prefix_keys.shape[0] * n
    lanes = jnp.arange(128, dtype=jnp.int32)
    picked = routes[:, :, None] == lanes[None, None, :]
    gates = jnp.sum(jnp.where(picked, gate_scores[:, :, None], 0.0), axis=1)
    kv_all, gate_all = gather(
        n, jnp.concatenate([cached_prefix_keys, cached_prefix_values], axis=1), gates
    )
    kv_all = kv_all.reshape(prefix_len, 2 * kv_width)

    doc_row = doc_ids[0]
    row_index = jnp.arange(rows_dev, dtype=jnp.int32)
    same_doc = doc_row[:, None] == doc_row[None, :]
    doc_start = jnp.min(jnp.where(same_doc, row_index[None, :], rows_dev), axis=1)
    token_positions = (prefix_len + row_index - doc_start).astype(F32)
    normed_input = normalize(hidden_in).astype(BF16)
    query_rows_all = jnp.dot(normed_input, w_query, preferred_element_type=F32).reshape(
        rows_dev, kv_local * group_width, head_size
    )
    query_rows_all = (
        rotary_apply(query_rows_all, token_positions)
        .astype(BF16)
        .reshape(rows_dev, kv_local, group_width, head_size)
    )
    fresh_key = jnp.dot(normed_input, key_weight, preferred_element_type=F32).reshape(
        rows_dev, kv_local, head_size
    )
    fresh_key = rotary_apply(fresh_key, token_positions).astype(BF16)
    fresh_value = (
        jnp.dot(normed_input, value_weight, preferred_element_type=F32)
        .astype(BF16)
        .reshape(rows_dev, kv_local, head_size)
    )
    own_scores = (
        jnp.einsum("tkgd,skd->tkgs", query_rows_all, fresh_key, preferred_element_type=F32)
        / head_size
    )
    visible = same_doc & (row_index[None, :] <= row_index[:, None])
    own_scores = jnp.where(visible[:, None, None, :], own_scores, -jnp.inf)
    key_rows = kv_all[:, :kv_width].reshape(-1, kv_local, head_size)
    value_rows = kv_all[:, kv_width:].reshape(-1, kv_local, head_size)
    scores = (
        jnp.einsum("tkgd,pkd->tkgp", query_rows_all, key_rows, preferred_element_type=F32)
        / head_size
    )
    top = jnp.maximum(jnp.max(own_scores, axis=-1), jnp.max(scores, axis=-1))
    own_weights = jnp.exp(own_scores - top[..., None])
    weights = jnp.exp(scores - top[..., None])
    denominator = jnp.sum(own_weights, axis=-1) + jnp.sum(weights, axis=-1)
    numerator = jnp.einsum(
        "tkgs,skd->tkgd", own_weights.astype(BF16), fresh_value, preferred_element_type=F32
    ) + jnp.einsum("tkgp,pkd->tkgd", weights.astype(BF16), value_rows, preferred_element_type=F32)
    attended = (
        (numerator / denominator[..., None])
        .astype(BF16)
        .reshape(rows_dev, kv_local * group_width * head_size)
    )
    return tail(n, n_tp, attended, w_out, hidden_in, gate_all, expert_in, expert_out)


def solution(mesh):
    in_specs = (
        P("seq", None),
        P(None, "tp"),
        P(None, "tp"),
        P(None, "tp"),
        P("tp", None),
        P("seq", "tp"),
        P("seq", "tp"),
        P("seq", None),
        P(("seq", "tp"), None),
        P(("seq", "tp"), None),
        P("seq", None, None),
        P("seq", None, None),
    )
    out_specs = (P(("seq", "tp"), None), P(("seq", "tp"), None), P(("seq", "tp"), None))
    return jax.shard_map(body, mesh=mesh, in_specs=in_specs, out_specs=out_specs, check_vma=False)
```

```python
import functools

import jax
import jax.numpy as jnp
from jax import lax
from jax.experimental import pallas as pl
from jax.experimental.pallas import tpu as pltpu
from jax.sharding import PartitionSpec as P

HEAD_WIDTH = 64
EXPERTS = 32
EPSILON = 1e-06
RESIDUAL = 0.22
MESH = pl.DeviceIdType.MESH
F32 = jnp.float32
BF16 = jnp.bfloat16


def normalize(values):
    values = values.astype(F32)
    return values * lax.rsqrt(jnp.mean(values * values, axis=-1, keepdims=True) + EPSILON)


def each(start, stop, fn):
    if stop - start <= 8:
        for i in range(start, stop):
            fn(i)
    else:

        @pl.loop(start, stop)
        def _(i):
            fn(i)


def peers(n):
    half = n // 2
    me = lax.axis_index("seq")
    high, low = me // 2, lax.rem(me, 2)

    def ahead(side, step):
        place = low if side == 0 else 1 - low
        return {"seq": lax.rem(high + step, half) * 2 + place}

    def behind(side, step):
        place = low if side == 0 else 1 - low
        return {"seq": lax.rem(high + half - step, half) * 2 + place}

    return half, ahead, behind


def attend_kernel(
    n,
    hidden, key_own, value_own, docs, routes, scores, wq_hbm, wk_hbm, wv_hbm,
    attended, gate_all,
    wq, wk, wv, packed, key_all, value_all, gates_in, w_sem, send, recv,
):
    half, ahead, _ = peers(n)
    block = hidden.shape[0]
    rows = routes.shape[0]
    share = key_own.shape[0]
    head_size = HEAD_WIDTH
    kv_local = wk.shape[1] // head_size
    group = wq.shape[1] // wk.shape[1]
    fetches = [
        pltpu.make_async_copy(src, dst, w_sem.at[i])
        for i, (src, dst) in enumerate(((wq_hbm, wq), (wk_hbm, wk), (wv_hbm, wv)))
    ]
    for f in fetches:
        f.start()
    barrier = pltpu.get_barrier_semaphore()

    def greet(side, step):
        pl.semaphore_signal(barrier, inc=1, device_id=ahead(side, step), device_id_type=MESH)

    each(1, half, lambda step: greet(0, step))
    each(0, half, lambda step: greet(1, step))

    lanes_g = lax.broadcasted_iota(jnp.int32, (rows, 128), 1)
    dense = jnp.zeros((rows, 128), F32)
    for k in range(routes.shape[1]):
        dense = dense + jnp.where(lanes_g == routes[:, k : k + 1], scores[:, k : k + 1], 0.0)
    tile = dense[0:8]
    for i in range(1, rows // 8):
        tile = tile + pltpu.roll(dense[8 * i : 8 * i + 8], 32 * i, 1)
    packed[...] = tile
    gates_in[0] = tile
    key_all[0] = key_own[...]
    value_all[0] = value_own[...]
    pl.semaphore_wait(barrier, n - 1)

    def copies(side, step):
        slot = side * half + step
        pairs = ((key_own, key_all), (value_own, value_all), (packed, gates_in))
        return [
            pltpu.make_async_remote_copy(
                src_ref=src,
                dst_ref=dst.at[slot],
                send_sem=send.at[kind, slot],
                recv_sem=recv.at[kind, slot],
                device_id=ahead(side, step),
                device_id_type=MESH,
            )
            for kind, (src, dst) in enumerate(pairs)
        ]

    def start(side, step):
        for c in copies(side, step):
            c.start()

    def finish(side, step):
        for c in copies(side, step):
            c.wait()

    each(1, half, lambda step: start(0, step))
    each(0, half, lambda step: start(1, step))

    normed = normalize(hidden[...]).astype(BF16)
    doc = jnp.broadcast_to(docs[...].astype(F32), (block, block))
    lane = lax.broadcasted_iota(jnp.int32, (block, block), 1)
    row = lax.broadcasted_iota(jnp.int32, (block, block), 0)
    same = doc == doc.T
    first = jnp.min(jnp.where(same, lane, block).astype(F32), axis=1, keepdims=True)
    positions = (share * n + row).astype(F32) - first
    pair = lax.broadcasted_iota(jnp.int32, (block, 128), 1)
    low_half = lax.rem(pair, head_size) < head_size // 2
    place = lax.rem(pair, head_size // 2).astype(F32)
    frequency = jnp.exp(-jnp.log(jnp.float32(10000.0)) * place * 2.0 / head_size)
    angles = positions[:, :1] * frequency
    cosine = jnp.cos(angles)
    sine = jnp.sin(angles)
    sine = jnp.where(low_half, -sine, sine)

    def rope(x):
        turned = jnp.where(
            low_half,
            pltpu.roll(x, 128 - head_size // 2, 1),
            pltpu.roll(x, head_size // 2, 1),
        )
        return (x * cosine + turned * sine).astype(BF16)

    def heads(x):
        return [x[:, j * head_size : (j + 1) * head_size] for j in range(128 // head_size)]

    def roped_heads(x):
        return [h for j in range(x.shape[1] // 128) for h in heads(rope(x[:, j * 128 : j * 128 + 128]))]

    for f in fetches:
        f.wait()
    q = roped_heads(jnp.dot(normed, wq[...], preferred_element_type=F32))
    k = roped_heads(jnp.dot(normed, wk[...], preferred_element_type=F32))
    v = jnp.dot(normed, wv[...], preferred_element_type=F32).astype(BF16)
    v = [v[:, j * head_size : (j + 1) * head_size] for j in range(kv_local)]
    visible = same & (lane <= row)
    visible = jnp.concatenate([visible.astype(F32)] * group, axis=0) > 0.5
    contract = (((1,), (1,)), ((), ()))
    states = []
    queries = []
    for g in range(kv_local):
        query = jnp.concatenate(q[g * group : (g + 1) * group], axis=0)
        own = lax.dot_general(query, k[g], contract, preferred_element_type=F32) / head_size
        own = jnp.where(visible, own, -jnp.inf)
        top = jnp.max(own, axis=1, keepdims=True)
        weights = jnp.exp(own - top)
        total = jnp.sum(weights, axis=1, keepdims=True)
        mixed = jnp.dot(weights.astype(BF16), v[g], preferred_element_type=F32)
        queries.append(query)
        states += [top, total, mixed]

    each(1, half, lambda step: finish(0, step))
    each(0, half, lambda step: finish(1, step))

    span = 8 if n % 8 == 0 else n

    def prefix(begin, carry):
        keys = key_all[pl.ds(begin, span)].reshape(span * share, kv_local * head_size)
        values = value_all[pl.ds(begin, span)].reshape(span * share, kv_local * head_size)
        out = []
        for g in range(kv_local):
            top, total, mixed = carry[3 * g : 3 * g + 3]
            mine = slice(g * head_size, (g + 1) * head_size)
            sc = lax.dot_general(queries[g], keys[:, mine], contract, preferred_element_type=F32)
            sc = sc / head_size
            higher = jnp.maximum(top, jnp.max(sc, axis=1, keepdims=True))
            shrink = jnp.exp(top - higher)
            weights = jnp.exp(sc - higher)
            total = total * shrink + jnp.sum(weights, axis=1, keepdims=True)
            mixed = mixed * shrink + jnp.dot(
                weights.astype(BF16), values[:, mine], preferred_element_type=F32
            )
            out += [higher, total, mixed]
        return tuple(out)

    if n == span:
        states = prefix(0, tuple(states))
    else:
        states = lax.fori_loop(0, n // span, lambda c, s: prefix(c * span, s), tuple(states))
    done = []
    for g in range(kv_local):
        _, total, mixed = states[3 * g : 3 * g + 3]
        result = mixed / total
        done += [result[j * block : (j + 1) * block] for j in range(group)]
    attended[...] = jnp.concatenate(done, axis=1).astype(BF16)

    def unpack(slot):
        t = gates_in[slot]
        gate_all[slot, 0:8] = t
        for i in range(1, rows // 8):
            gate_all[slot, 8 * i : 8 * i + 8] = pltpu.roll(t, 128 - 32 * i, 1)

    each(0, n, unpack)


def attend(n, hidden, key_own, value_own, docs, routes, scores, w_query, key_weight, value_weight):
    vmem = pl.BlockSpec(memory_space=pltpu.VMEM)
    hbm = pl.BlockSpec(memory_space=pl.ANY)
    rows = routes.shape[0]
    return pl.pallas_call(
        functools.partial(attend_kernel, n),
        out_shape=(
            jax.ShapeDtypeStruct((hidden.shape[0], w_query.shape[1]), BF16),
            jax.ShapeDtypeStruct((n, rows, 128), F32),
        ),
        in_specs=[vmem] * 6 + [hbm] * 3,
        out_specs=(vmem, vmem),
        scratch_shapes=[
            pltpu.VMEM(w_query.shape, BF16),
            pltpu.VMEM(key_weight.shape, BF16),
            pltpu.VMEM(value_weight.shape, BF16),
            pltpu.VMEM((8, 128), F32),
            pltpu.VMEM((n,) + key_own.shape, BF16),
            pltpu.VMEM((n,) + value_own.shape, BF16),
            pltpu.VMEM((n, 8, 128), F32),
            pltpu.SemaphoreType.DMA((3,)),
            pltpu.SemaphoreType.DMA((3, n)),
            pltpu.SemaphoreType.DMA((3, n)),
        ],
        compiler_params=pltpu.CompilerParams(
            collective_id=0, has_side_effects=True, vmem_limit_bytes=40 << 20
        ),
    )(hidden, key_own, value_own, docs, routes, scores, w_query, key_weight, value_weight)


def tail_kernel(
    n, n_tp, hparts,
    attended, hidden, gate_all, w_out_hbm, in_hbm, out_hbm,
    proj_ref, mix_ref, layer_ref,
    w_out, w_in, w_back, sums, outbox, inbox, tok, part, acc, cross, cross_in, home, home_in,
    o_sem, w_sem, tp_send, tp_recv, tok_send, tok_recv, x_send, x_recv, h_send, h_recv,
):
    half, ahead, behind = peers(n)
    units, ff = out_hbm.shape[0], out_hbm.shape[1]
    rows, width = proj_ref.shape
    me_tp = lax.axis_index("tp")
    chunk = min(4, half)

    def fetch(u):
        return (
            pltpu.make_async_copy(in_hbm.at[u], w_in.at[u], w_sem.at[0, u]),
            pltpu.make_async_copy(out_hbm.at[u], w_back.at[u], w_sem.at[1, u]),
        )

    out_fetch = pltpu.make_async_copy(w_out_hbm, w_out, o_sem)
    out_fetch.start()
    barrier = pltpu.get_barrier_semaphore()

    def greet(where):
        pl.semaphore_signal(barrier, inc=1, device_id=where, device_id_type=MESH)

    def tp_peer(t):
        return lax.rem(me_tp + t, n_tp)

    each(1, n_tp, lambda t: greet({"tp": tp_peer(t)}))
    each(1, half, lambda d: greet(ahead(0, d)))
    greet(ahead(1, 0))
    for u in range(units):
        for c in fetch(u):
            c.start()
    out_fetch.wait()
    whole = jnp.dot(attended[...], w_out[...], preferred_element_type=F32)
    sums[...] = whole
    outbox[...] = whole.astype(BF16)
    pl.semaphore_wait(barrier, n_tp - 1 + half)

    def tp_copy(t):
        return pltpu.make_async_remote_copy(
            src_ref=outbox.at[pl.ds(pl.multiple_of(tp_peer(t) * rows, rows), rows)],
            dst_ref=inbox.at[t],
            send_sem=tp_send.at[t],
            recv_sem=tp_recv.at[t],
            device_id={"tp": tp_peer(t)},
            device_id_type=MESH,
        )

    each(1, n_tp, lambda t: tp_copy(t).start())
    mine = pl.ds(pl.multiple_of(me_tp * rows, rows), rows)
    attn_sum = sums[mine, :]
    for t in range(1, n_tp):
        tp_copy(t).wait_recv()
        attn_sum = attn_sum + inbox[t].astype(F32)
    residual = hidden[mine, :].astype(F32) + RESIDUAL * attn_sum
    proj_ref[...] = attn_sum.astype(BF16)
    tok[0, 0] = normalize(residual).astype(BF16)

    def tok_copy(d):
        return pltpu.make_async_remote_copy(
            src_ref=tok.at[0, 0],
            dst_ref=tok.at[0, d],
            send_sem=tok_send.at[0, d],
            recv_sem=tok_recv.at[0, d],
            device_id=ahead(0, d),
            device_id_type=MESH,
        )

    def tok_cross(d):
        return pltpu.make_async_remote_copy(
            src_ref=tok.at[0, d],
            dst_ref=tok.at[1, d],
            send_sem=tok_send.at[1, d],
            recv_sem=tok_recv.at[1, d],
            device_id=ahead(1, 0),
            device_id_type=MESH,
        )

    def relay(d):
        tok_copy(d).wait_recv()
        tok_cross(d).start()

    each(1, half, lambda d: tok_copy(d).start())
    tok_cross(0).start()
    for u in range(units):
        for c in fetch(u):
            c.wait()
    each(1, half, relay)

    first_unit = lax.axis_index("seq") * units

    def experts(side, begin):
        tokens = tok[side, pl.ds(begin, chunk)].reshape(chunk * rows, width)
        gates = gate_all[pl.ds(side * half + begin, chunk)].reshape(chunk * rows, gate_all.shape[-1])
        lanes = lax.broadcasted_iota(jnp.int32, gates.shape, 1)
        acc[...] = jnp.zeros(acc.shape, F32)

        @pl.loop(0, units)
        def _(u):
            expert = (first_unit + u) // hparts
            weight = jnp.sum(jnp.where(lanes == expert, gates, 0.0), axis=1, keepdims=True)
            gate_up = jnp.dot(tokens, w_in[u], preferred_element_type=F32)
            active = (jax.nn.silu(gate_up[:, :ff]) * gate_up[:, ff:]).astype(BF16)
            back = jnp.dot(active, w_back[u], preferred_element_type=F32).astype(BF16)
            acc[...] += weight * back.astype(F32)

        total = acc[...].reshape(chunk, rows, width)
        if side == 0:
            part[pl.ds(begin, chunk)] = total
        else:
            cross[pl.ds(begin, chunk)] = total.astype(BF16)

    each(0, half // chunk, lambda c: experts(0, c * chunk))

    def cross_copy(d):
        return pltpu.make_async_remote_copy(
            src_ref=cross.at[d],
            dst_ref=cross_in.at[d],
            send_sem=x_send.at[d],
            recv_sem=x_recv.at[d],
            device_id=ahead(1, 0),
            device_id_type=MESH,
        )

    def send_cross(d):
        cross_copy(d).start()

    each(0, half, lambda d: tok_cross(d).wait_recv())
    each(0, half // chunk, lambda c: experts(1, c * chunk))
    each(1, half, send_cross)
    send_cross(0)

    def home_copy(d):
        return pltpu.make_async_remote_copy(
            src_ref=home.at[d],
            dst_ref=home_in.at[d],
            send_sem=h_send.at[d],
            recv_sem=h_recv.at[d],
            device_id=behind(0, d),
            device_id_type=MESH,
        )

    def send_home(d):
        cross_copy(d).wait_recv()
        home[d] = (part[d] + cross_in[d].astype(F32)).astype(BF16)
        home_copy(d).start()

    each(1, half, send_home)
    cross_copy(0).wait_recv()
    part[0] += cross_in[0].astype(F32)

    def collect(d):
        home_copy(d).wait_recv()
        part[0] += home_in[d].astype(F32)

    each(1, half, collect)
    expert_sum = part[0]
    mix_ref[...] = expert_sum.astype(BF16)
    layer_ref[...] = (residual + RESIDUAL * expert_sum).astype(BF16)

    each(1, n_tp, lambda t: tp_copy(t).wait_send())
    each(1, half, lambda d: tok_copy(d).wait_send())
    each(0, half, lambda d: tok_cross(d).wait_send())
    each(0, half, lambda d: cross_copy(d).wait_send())
    each(1, half, lambda d: home_copy(d).wait_send())


def tail(n, n_tp, attended, w_out, hidden, gate_all, expert_in, expert_out):
    half = n // 2
    block, width = hidden.shape
    rows = block // n_tp
    units, ff = expert_out.shape[:2]
    hparts = units * n // EXPERTS
    vmem = pl.BlockSpec(memory_space=pltpu.VMEM)
    hbm = pl.BlockSpec(memory_space=pl.ANY)
    out = jax.ShapeDtypeStruct((rows, width), BF16)
    dma = pltpu.SemaphoreType.DMA
    return pl.pallas_call(
        functools.partial(tail_kernel, n, n_tp, hparts),
        out_shape=(out, out, out),
        in_specs=[vmem, vmem, vmem, hbm, hbm, hbm],
        out_specs=(vmem, vmem, vmem),
        scratch_shapes=[
            pltpu.VMEM(w_out.shape, BF16),
            pltpu.VMEM(expert_in.shape, BF16),
            pltpu.VMEM(expert_out.shape, BF16),
            pltpu.VMEM((block, width), F32),
            pltpu.VMEM((block, width), BF16),
            pltpu.VMEM((n_tp, rows, width), BF16),
            pltpu.VMEM((2, half, rows, width), BF16),
            pltpu.VMEM((half, rows, width), F32),
            pltpu.VMEM((min(4, half) * rows, width), F32),
            pltpu.VMEM((half, rows, width), BF16),
            pltpu.VMEM((half, rows, width), BF16),
            pltpu.VMEM((half, rows, width), BF16),
            pltpu.VMEM((half, rows, width), BF16),
            dma,
            dma((2, units)),
            dma((n_tp,)),
            dma((n_tp,)),
            dma((2, half)),
            dma((2, half)),
            dma((half,)),
            dma((half,)),
            dma((half,)),
            dma((half,)),
        ],
        compiler_params=pltpu.CompilerParams(
            collective_id=1,
            has_side_effects=True,
            vmem_limit_bytes=(44 << 20) if half <= 8 else (63 << 20),
        ),
    )(attended, hidden, gate_all, w_out, expert_in, expert_out)


def body(
    hidden_in,
    w_query,
    key_weight,
    value_weight,
    w_out,
    cached_prefix_keys,
    cached_prefix_values,
    doc_ids,
    routes,
    gate_scores,
    expert_in,
    expert_out,
):
    n, n_tp = lax.axis_size("seq"), lax.axis_size("tp")
    attended, gate_all = attend(
        n, hidden_in, cached_prefix_keys, cached_prefix_values, doc_ids, routes, gate_scores,
        w_query, key_weight, value_weight,
    )
    return tail(n, n_tp, attended, w_out, hidden_in, gate_all, expert_in, expert_out)


def solution(mesh):
    in_specs = (
        P("seq", None),
        P(None, "tp"),
        P(None, "tp"),
        P(None, "tp"),
        P("tp", None),
        P("seq", "tp"),
        P("seq", "tp"),
        P("seq", None),
        P(("seq", "tp"), None),
        P(("seq", "tp"), None),
        P("seq", None, None),
        P("seq", None, None),
    )
    out_specs = (P(("seq", "tp"), None), P(("seq", "tp"), None), P(("seq", "tp"), None))
    return jax.shard_map(body, mesh=mesh, in_specs=in_specs, out_specs=out_specs, check_vma=False)
```

```python
import functools

import jax
import jax.numpy as jnp
from jax import lax
from jax.experimental import pallas as pl
from jax.experimental.pallas import tpu as pltpu
from jax.sharding import PartitionSpec as P

HEAD_WIDTH = 64
EXPERTS = 32
EPSILON = 1e-06
RESIDUAL = 0.22
MESH = pl.DeviceIdType.MESH
F32 = jnp.float32
BF16 = jnp.bfloat16


def normalize(values):
    values = values.astype(F32)
    return values * lax.rsqrt(jnp.mean(values * values, axis=-1, keepdims=True) + EPSILON)


def each(start, stop, fn):
    if stop - start <= 8:
        for i in range(start, stop):
            fn(i)
    else:

        @pl.loop(start, stop)
        def _(i):
            fn(i)


def peers(n):
    half = n // 2
    me = lax.axis_index("seq")
    high, low = me // 2, lax.rem(me, 2)

    def ahead(side, step):
        place = low if side == 0 else 1 - low
        return {"seq": lax.rem(high + step, half) * 2 + place}

    def behind(side, step):
        place = low if side == 0 else 1 - low
        return {"seq": lax.rem(high + half - step, half) * 2 + place}

    return half, ahead, behind


def attend_kernel(
    n,
    hidden, key_own, value_own, docs, routes, scores, wq_hbm, wk_hbm, wv_hbm,
    attended, gate_all,
    wq, wk, wv, packed, key_all, value_all, gates_in, w_sem, send, recv,
):
    half, ahead, _ = peers(n)
    block = hidden.shape[0]
    rows = routes.shape[0]
    share = key_own.shape[0]
    head_size = HEAD_WIDTH
    kv_local = wk.shape[1] // head_size
    group = wq.shape[1] // wk.shape[1]
    fetches = [
        pltpu.make_async_copy(src, dst, w_sem.at[i])
        for i, (src, dst) in enumerate(((wq_hbm, wq), (wk_hbm, wk), (wv_hbm, wv)))
    ]
    for f in fetches:
        f.start()
    barrier = pltpu.get_barrier_semaphore()

    def greet(side, step):
        pl.semaphore_signal(barrier, inc=1, device_id=ahead(side, step), device_id_type=MESH)

    each(1, half, lambda step: greet(0, step))
    each(0, half, lambda step: greet(1, step))

    lanes_g = lax.broadcasted_iota(jnp.int32, (rows, 128), 1)
    dense = jnp.zeros((rows, 128), F32)
    for k in range(routes.shape[1]):
        dense = dense + jnp.where(lanes_g == routes[:, k : k + 1], scores[:, k : k + 1], 0.0)
    tile = dense[0:8]
    for i in range(1, rows // 8):
        tile = tile + pltpu.roll(dense[8 * i : 8 * i + 8], 32 * i, 1)
    packed[...] = tile
    gates_in[0] = tile
    key_all[0] = key_own[...]
    value_all[0] = value_own[...]
    pl.semaphore_wait(barrier, n - 1)

    def copies(side, step):
        slot = side * half + step
        pairs = ((key_own, key_all), (value_own, value_all), (packed, gates_in))
        return [
            pltpu.make_async_remote_copy(
                src_ref=src,
                dst_ref=dst.at[slot],
                send_sem=send.at[kind, slot],
                recv_sem=recv.at[kind, slot],
                device_id=ahead(side, step),
                device_id_type=MESH,
            )
            for kind, (src, dst) in enumerate(pairs)
        ]

    def start(side, step):
        for c in copies(side, step):
            c.start()

    def finish(side, step):
        for c in copies(side, step):
            c.wait()

    each(1, half, lambda step: start(0, step))
    each(0, half, lambda step: start(1, step))

    normed = normalize(hidden[...]).astype(BF16)
    doc = jnp.broadcast_to(docs[...].astype(F32), (block, block))
    lane = lax.broadcasted_iota(jnp.int32, (block, block), 1)
    row = lax.broadcasted_iota(jnp.int32, (block, block), 0)
    same = doc == doc.T
    first = jnp.min(jnp.where(same, lane, block).astype(F32), axis=1, keepdims=True)
    positions = (share * n + row).astype(F32) - first
    pair = lax.broadcasted_iota(jnp.int32, (block, 128), 1)
    low_half = lax.rem(pair, head_size) < head_size // 2
    place = lax.rem(pair, head_size // 2).astype(F32)
    frequency = jnp.exp(-jnp.log(jnp.float32(10000.0)) * place * 2.0 / head_size)
    angles = positions[:, :1] * frequency
    cosine = jnp.cos(angles)
    sine = jnp.sin(angles)
    sine = jnp.where(low_half, -sine, sine)

    def rope(x):
        turned = jnp.where(
            low_half,
            pltpu.roll(x, 128 - head_size // 2, 1),
            pltpu.roll(x, head_size // 2, 1),
        )
        return (x * cosine + turned * sine).astype(BF16)

    def heads(x):
        return [x[:, j * head_size : (j + 1) * head_size] for j in range(128 // head_size)]

    def roped_heads(x):
        return [h for j in range(x.shape[1] // 128) for h in heads(rope(x[:, j * 128 : j * 128 + 128]))]

    for f in fetches:
        f.wait()
    q = roped_heads(jnp.dot(normed, wq[...], preferred_element_type=F32))
    k = roped_heads(jnp.dot(normed, wk[...], preferred_element_type=F32))
    v = jnp.dot(normed, wv[...], preferred_element_type=F32).astype(BF16)
    v = [v[:, j * head_size : (j + 1) * head_size] for j in range(kv_local)]
    visible = same & (lane <= row)
    visible = jnp.concatenate([visible.astype(F32)] * group, axis=0) > 0.5
    contract = (((1,), (1,)), ((), ()))
    states = []
    queries = []
    for g in range(kv_local):
        query = jnp.concatenate(q[g * group : (g + 1) * group], axis=0)
        own = lax.dot_general(query, k[g], contract, preferred_element_type=F32) / head_size
        own = jnp.where(visible, own, -jnp.inf)
        top = jnp.max(own, axis=1, keepdims=True)
        weights = jnp.exp(own - top)
        total = jnp.sum(weights, axis=1, keepdims=True)
        mixed = jnp.dot(weights.astype(BF16), v[g], preferred_element_type=F32)
        queries.append(query)
        states += [top, total, mixed]

    each(1, half, lambda step: finish(0, step))
    each(0, half, lambda step: finish(1, step))

    span = 8 if n % 8 == 0 else n

    def prefix(begin, carry):
        keys = key_all[pl.ds(begin, span)].reshape(span * share, kv_local * head_size)
        values = value_all[pl.ds(begin, span)].reshape(span * share, kv_local * head_size)
        out = []
        for g in range(kv_local):
            top, total, mixed = carry[3 * g : 3 * g + 3]
            mine = slice(g * head_size, (g + 1) * head_size)
            sc = lax.dot_general(queries[g], keys[:, mine], contract, preferred_element_type=F32)
            sc = sc / head_size
            higher = jnp.maximum(top, jnp.max(sc, axis=1, keepdims=True))
            shrink = jnp.exp(top - higher)
            weights = jnp.exp(sc - higher)
            total = total * shrink + jnp.sum(weights, axis=1, keepdims=True)
            mixed = mixed * shrink + jnp.dot(
                weights.astype(BF16), values[:, mine], preferred_element_type=F32
            )
            out += [higher, total, mixed]
        return tuple(out)

    if n == span:
        states = prefix(0, tuple(states))
    else:
        states = lax.fori_loop(0, n // span, lambda c, s: prefix(c * span, s), tuple(states))
    done = []
    for g in range(kv_local):
        _, total, mixed = states[3 * g : 3 * g + 3]
        result = mixed / total
        done += [result[j * block : (j + 1) * block] for j in range(group)]
    attended[...] = jnp.concatenate(done, axis=1).astype(BF16)

    def unpack(slot):
        t = gates_in[slot]
        gate_all[slot, 0:8] = t
        for i in range(1, rows // 8):
            gate_all[slot, 8 * i : 8 * i + 8] = pltpu.roll(t, 128 - 32 * i, 1)

    each(0, n, unpack)


def attend(n, hidden, key_own, value_own, docs, routes, scores, w_query, key_weight, value_weight):
    vmem = pl.BlockSpec(memory_space=pltpu.VMEM)
    hbm = pl.BlockSpec(memory_space=pltpu.HBM)
    rows = routes.shape[0]
    return pl.pallas_call(
        functools.partial(attend_kernel, n),
        out_shape=(
            jax.ShapeDtypeStruct((hidden.shape[0], w_query.shape[1]), BF16),
            jax.ShapeDtypeStruct((n, rows, 128), F32),
        ),
        in_specs=[vmem] * 6 + [hbm] * 3,
        out_specs=(vmem, vmem),
        scratch_shapes=[
            pltpu.VMEM(w_query.shape, BF16),
            pltpu.VMEM(key_weight.shape, BF16),
            pltpu.VMEM(value_weight.shape, BF16),
            pltpu.VMEM((8, 128), F32),
            pltpu.VMEM((n,) + key_own.shape, BF16),
            pltpu.VMEM((n,) + value_own.shape, BF16),
            pltpu.VMEM((n, 8, 128), F32),
            pltpu.SemaphoreType.DMA((3,)),
            pltpu.SemaphoreType.DMA((3, n)),
            pltpu.SemaphoreType.DMA((3, n)),
        ],
        compiler_params=pltpu.CompilerParams(
            collective_id=0, has_side_effects=True, vmem_limit_bytes=60 << 20
        ),
    )(hidden, key_own, value_own, docs, routes, scores, w_query, key_weight, value_weight)


def tail_kernel(
    n, n_tp, hparts,
    attended, hidden, gate_all, w_out_hbm, in_hbm, out_hbm,
    proj_ref, mix_ref, layer_ref,
    w_out, w_in, w_back, sums, outbox, inbox, tok, part, acc, cross, cross_in, home, home_in,
    o_sem, w_sem, tp_send, tp_recv, tok_send, tok_recv, x_send, x_recv, h_send, h_recv,
):
    half, ahead, behind = peers(n)
    units, ff = out_hbm.shape[0], out_hbm.shape[1]
    rows, width = proj_ref.shape
    me_tp = lax.axis_index("tp")
    chunk = min(4, half)

    def fetch(u):
        return (
            pltpu.make_async_copy(in_hbm.at[u], w_in.at[u], w_sem.at[0, u]),
            pltpu.make_async_copy(out_hbm.at[u], w_back.at[u], w_sem.at[1, u]),
        )

    out_fetch = pltpu.make_async_copy(w_out_hbm, w_out, o_sem)
    out_fetch.start()
    barrier = pltpu.get_barrier_semaphore()

    def greet(where):
        pl.semaphore_signal(barrier, inc=1, device_id=where, device_id_type=MESH)

    def tp_peer(t):
        return lax.rem(me_tp + t, n_tp)

    each(1, n_tp, lambda t: greet({"tp": tp_peer(t)}))
    each(1, half, lambda d: greet(ahead(0, d)))
    greet(ahead(1, 0))
    for u in range(units):
        for c in fetch(u):
            c.start()
    out_fetch.wait()
    whole = jnp.dot(attended[...], w_out[...], preferred_element_type=F32)
    sums[...] = whole
    outbox[...] = whole.astype(BF16)
    pl.semaphore_wait(barrier, n_tp - 1 + half)

    def tp_copy(t):
        return pltpu.make_async_remote_copy(
            src_ref=outbox.at[pl.ds(pl.multiple_of(tp_peer(t) * rows, rows), rows)],
            dst_ref=inbox.at[t],
            send_sem=tp_send.at[t],
            recv_sem=tp_recv.at[t],
            device_id={"tp": tp_peer(t)},
            device_id_type=MESH,
        )

    each(1, n_tp, lambda t: tp_copy(t).start())
    mine = pl.ds(pl.multiple_of(me_tp * rows, rows), rows)
    attn_sum = sums[mine, :]
    for t in range(1, n_tp):
        tp_copy(t).wait_recv()
        attn_sum = attn_sum + inbox[t].astype(F32)
    residual = hidden[mine, :].astype(F32) + RESIDUAL * attn_sum
    proj_ref[...] = attn_sum.astype(BF16)
    tok[0, 0] = normalize(residual).astype(BF16)

    def tok_copy(d):
        return pltpu.make_async_remote_copy(
            src_ref=tok.at[0, 0],
            dst_ref=tok.at[0, d],
            send_sem=tok_send.at[0, d],
            recv_sem=tok_recv.at[0, d],
            device_id=ahead(0, d),
            device_id_type=MESH,
        )

    def tok_cross(d):
        return pltpu.make_async_remote_copy(
            src_ref=tok.at[0, d],
            dst_ref=tok.at[1, d],
            send_sem=tok_send.at[1, d],
            recv_sem=tok_recv.at[1, d],
            device_id=ahead(1, 0),
            device_id_type=MESH,
        )

    def relay(d):
        tok_copy(d).wait_recv()
        tok_cross(d).start()

    each(1, half, lambda d: tok_copy(d).start())
    tok_cross(0).start()
    for u in range(units):
        for c in fetch(u):
            c.wait()
    each(1, half, relay)

    first_unit = lax.axis_index("seq") * units

    def experts(side, begin):
        tokens = tok[side, pl.ds(begin, chunk)].reshape(chunk * rows, width)
        gates = gate_all[pl.ds(side * half + begin, chunk)].reshape(chunk * rows, gate_all.shape[-1])
        lanes = lax.broadcasted_iota(jnp.int32, gates.shape, 1)
        acc[...] = jnp.zeros(acc.shape, F32)

        @pl.loop(0, units)
        def _(u):
            expert = (first_unit + u) // hparts
            weight = jnp.sum(jnp.where(lanes == expert, gates, 0.0), axis=1, keepdims=True)
            gate_up = jnp.dot(tokens, w_in[u], preferred_element_type=F32)
            active = (jax.nn.silu(gate_up[:, :ff]) * gate_up[:, ff:]).astype(BF16)
            back = jnp.dot(active, w_back[u], preferred_element_type=F32).astype(BF16)
            acc[...] += weight * back.astype(F32)

        total = acc[...].reshape(chunk, rows, width)
        if side == 0:
            part[pl.ds(begin, chunk)] = total
        else:
            cross[pl.ds(begin, chunk)] = total.astype(BF16)

    each(0, half // chunk, lambda c: experts(0, c * chunk))

    def cross_copy(d):
        return pltpu.make_async_remote_copy(
            src_ref=cross.at[d],
            dst_ref=cross_in.at[d],
            send_sem=x_send.at[d],
            recv_sem=x_recv.at[d],
            device_id=ahead(1, 0),
            device_id_type=MESH,
        )

    def send_cross(d):
        cross_copy(d).start()

    each(0, half, lambda d: tok_cross(d).wait_recv())
    each(0, half // chunk, lambda c: experts(1, c * chunk))
    each(1, half, send_cross)
    send_cross(0)

    def home_copy(d):
        return pltpu.make_async_remote_copy(
            src_ref=home.at[d],
            dst_ref=home_in.at[d],
            send_sem=h_send.at[d],
            recv_sem=h_recv.at[d],
            device_id=behind(0, d),
            device_id_type=MESH,
        )

    def send_home(d):
        cross_copy(d).wait_recv()
        home[d] = (part[d] + cross_in[d].astype(F32)).astype(BF16)
        home_copy(d).start()

    each(1, half, send_home)
    cross_copy(0).wait_recv()
    part[0] += cross_in[0].astype(F32)

    def collect(d):
        home_copy(d).wait_recv()
        part[0] += home_in[d].astype(F32)

    each(1, half, collect)
    expert_sum = part[0]
    mix_ref[...] = expert_sum.astype(BF16)
    layer_ref[...] = (residual + RESIDUAL * expert_sum).astype(BF16)

    each(1, n_tp, lambda t: tp_copy(t).wait_send())
    each(1, half, lambda d: tok_copy(d).wait_send())
    each(0, half, lambda d: tok_cross(d).wait_send())
    each(0, half, lambda d: cross_copy(d).wait_send())
    each(1, half, lambda d: home_copy(d).wait_send())


def tail(n, n_tp, attended, w_out, hidden, gate_all, expert_in, expert_out):
    half = n // 2
    block, width = hidden.shape
    rows = block // n_tp
    units, ff = expert_out.shape[:2]
    hparts = units * n // EXPERTS
    vmem = pl.BlockSpec(memory_space=pltpu.VMEM)
    hbm = pl.BlockSpec(memory_space=pltpu.HBM)
    out = jax.ShapeDtypeStruct((rows, width), BF16)
    dma = pltpu.SemaphoreType.DMA
    return pl.pallas_call(
        functools.partial(tail_kernel, n, n_tp, hparts),
        out_shape=(out, out, out),
        in_specs=[vmem, vmem, vmem, hbm, hbm, hbm],
        out_specs=(vmem, vmem, vmem),
        scratch_shapes=[
            pltpu.VMEM(w_out.shape, BF16),
            pltpu.VMEM(expert_in.shape, BF16),
            pltpu.VMEM(expert_out.shape, BF16),
            pltpu.VMEM((block, width), F32),
            pltpu.VMEM((block, width), BF16),
            pltpu.VMEM((n_tp, rows, width), BF16),
            pltpu.VMEM((2, half, rows, width), BF16),
            pltpu.VMEM((half, rows, width), F32),
            pltpu.VMEM((min(4, half) * rows, width), F32),
            pltpu.VMEM((half, rows, width), BF16),
            pltpu.VMEM((half, rows, width), BF16),
            pltpu.VMEM((half, rows, width), BF16),
            pltpu.VMEM((half, rows, width), BF16),
            dma,
            dma((2, units)),
            dma((n_tp,)),
            dma((n_tp,)),
            dma((2, half)),
            dma((2, half)),
            dma((half,)),
            dma((half,)),
            dma((half,)),
            dma((half,)),
        ],
        compiler_params=pltpu.CompilerParams(
            collective_id=1,
            has_side_effects=True,
            vmem_limit_bytes=62 << 20,
        ),
    )(attended, hidden, gate_all, w_out, expert_in, expert_out)


def body(
    hidden_in,
    w_query,
    key_weight,
    value_weight,
    w_out,
    cached_prefix_keys,
    cached_prefix_values,
    doc_ids,
    routes,
    gate_scores,
    expert_in,
    expert_out,
):
    n, n_tp = lax.axis_size("seq"), lax.axis_size("tp")
    attended, gate_all = attend(
        n, hidden_in, cached_prefix_keys, cached_prefix_values, doc_ids, routes, gate_scores,
        w_query, key_weight, value_weight,
    )
    return tail(n, n_tp, attended, w_out, hidden_in, gate_all, expert_in, expert_out)


def solution(mesh):
    in_specs = (
        P("seq", None),
        P(None, "tp"),
        P(None, "tp"),
        P(None, "tp"),
        P("tp", None),
        P("seq", "tp"),
        P("seq", "tp"),
        P("seq", None),
        P(("seq", "tp"), None),
        P(("seq", "tp"), None),
        P("seq", None, None),
        P("seq", None, None),
    )
    out_specs = (P(("seq", "tp"), None), P(("seq", "tp"), None), P(("seq", "tp"), None))
    return jax.shard_map(body, mesh=mesh, in_specs=in_specs, out_specs=out_specs, check_vma=False)
```

```python
import functools

import jax
import jax.numpy as jnp
from jax import lax
from jax.experimental import pallas as pl
from jax.experimental.pallas import tpu as pltpu
from jax.sharding import PartitionSpec as P

HEAD_WIDTH = 64
EXPERTS = 32
EPSILON = 1e-06
RESIDUAL = 0.22
MESH = pl.DeviceIdType.MESH
F32 = jnp.float32
BF16 = jnp.bfloat16


def normalize(values):
    values = values.astype(F32)
    return values * lax.rsqrt(jnp.mean(values * values, axis=-1, keepdims=True) + EPSILON)


def each(start, stop, fn):
    if stop - start <= 8:
        for i in range(start, stop):
            fn(i)
    else:

        @pl.loop(start, stop)
        def _(i):
            fn(i)


def peers(n):
    half = n // 2
    me = lax.axis_index("seq")
    high, low = me // 2, lax.rem(me, 2)

    def ahead(side, step):
        place = low if side == 0 else 1 - low
        return {"seq": lax.rem(high + step, half) * 2 + place}

    def behind(side, step):
        place = low if side == 0 else 1 - low
        return {"seq": lax.rem(high + half - step, half) * 2 + place}

    return half, ahead, behind


def attend_kernel(
    n,
    hidden, key_own, value_own, docs, gates, wq_hbm, wk_hbm, wv_hbm,
    attended, gate_all,
    wq, wk, wv, packed, key_all, value_all, gates_in, w_sem, send, recv,
):
    half, ahead, _ = peers(n)
    block = hidden.shape[0]
    rows = gate_all.shape[1]
    share = key_own.shape[0]
    head_size = HEAD_WIDTH
    kv_local = wk.shape[1] // head_size
    group = wq.shape[1] // wk.shape[1]
    fetches = [
        pltpu.make_async_copy(src, dst, w_sem.at[i])
        for i, (src, dst) in enumerate(((wq_hbm, wq), (wk_hbm, wk), (wv_hbm, wv)))
    ]
    for f in fetches:
        f.start()
    barrier = pltpu.get_barrier_semaphore()

    def greet(side, step):
        pl.semaphore_signal(barrier, inc=1, device_id=ahead(side, step), device_id_type=MESH)

    each(1, half, lambda step: greet(0, step))
    each(0, half, lambda step: greet(1, step))

    dense = gates[...].T[0:rows]
    tile = dense[0:8]
    for i in range(1, rows // 8):
        tile = tile + pltpu.roll(dense[8 * i : 8 * i + 8], 32 * i, 1)
    packed[...] = tile
    gates_in[0] = tile
    key_all[0] = key_own[...]
    value_all[0] = value_own[...]
    pl.semaphore_wait(barrier, n - 1)

    def copies(side, step):
        slot = side * half + step
        pairs = ((key_own, key_all), (value_own, value_all), (packed, gates_in))
        return [
            pltpu.make_async_remote_copy(
                src_ref=src,
                dst_ref=dst.at[slot],
                send_sem=send.at[kind, slot],
                recv_sem=recv.at[kind, slot],
                device_id=ahead(side, step),
                device_id_type=MESH,
            )
            for kind, (src, dst) in enumerate(pairs)
        ]

    def start(side, step):
        for c in copies(side, step):
            c.start()

    def finish(side, step):
        for c in copies(side, step):
            c.wait()

    each(1, half, lambda step: start(0, step))
    each(0, half, lambda step: start(1, step))

    normed = normalize(hidden[...]).astype(BF16)
    doc = jnp.broadcast_to(docs[...].astype(F32), (block, block))
    lane = lax.broadcasted_iota(jnp.int32, (block, block), 1)
    row = lax.broadcasted_iota(jnp.int32, (block, block), 0)
    same = doc == doc.T
    first = jnp.min(jnp.where(same, lane, block).astype(F32), axis=1, keepdims=True)
    positions = (share * n + row).astype(F32) - first
    pair = lax.broadcasted_iota(jnp.int32, (block, 128), 1)
    low_half = lax.rem(pair, head_size) < head_size // 2
    place = lax.rem(pair, head_size // 2).astype(F32)
    frequency = jnp.exp(-jnp.log(jnp.float32(10000.0)) * place * 2.0 / head_size)
    angles = positions[:, :1] * frequency
    cosine = jnp.cos(angles)
    sine = jnp.sin(angles)
    sine = jnp.where(low_half, -sine, sine)

    def rope(x):
        turned = jnp.where(
            low_half,
            pltpu.roll(x, 128 - head_size // 2, 1),
            pltpu.roll(x, head_size // 2, 1),
        )
        return (x * cosine + turned * sine).astype(BF16)

    def heads(x):
        return [x[:, j * head_size : (j + 1) * head_size] for j in range(128 // head_size)]

    def roped_heads(x):
        return [h for j in range(x.shape[1] // 128) for h in heads(rope(x[:, j * 128 : j * 128 + 128]))]

    for f in fetches:
        f.wait()
    q = roped_heads(jnp.dot(normed, wq[...], preferred_element_type=F32))
    k = roped_heads(jnp.dot(normed, wk[...], preferred_element_type=F32))
    v = jnp.dot(normed, wv[...], preferred_element_type=F32).astype(BF16)
    v = [v[:, j * head_size : (j + 1) * head_size] for j in range(kv_local)]
    visible = same & (lane <= row)
    visible = jnp.concatenate([visible.astype(F32)] * group, axis=0) > 0.5
    contract = (((1,), (1,)), ((), ()))
    states = []
    queries = []
    for g in range(kv_local):
        query = jnp.concatenate(q[g * group : (g + 1) * group], axis=0)
        own = lax.dot_general(query, k[g], contract, preferred_element_type=F32) / head_size
        own = jnp.where(visible, own, -jnp.inf)
        top = jnp.max(own, axis=1, keepdims=True)
        weights = jnp.exp(own - top)
        total = jnp.sum(weights, axis=1, keepdims=True)
        mixed = jnp.dot(weights.astype(BF16), v[g], preferred_element_type=F32)
        queries.append(query)
        states += [top, total, mixed]

    each(1, half, lambda step: finish(0, step))
    each(0, half, lambda step: finish(1, step))

    span = 8 if n % 8 == 0 else n

    def prefix(begin, carry):
        keys = key_all[pl.ds(begin, span)].reshape(span * share, kv_local * head_size)
        values = value_all[pl.ds(begin, span)].reshape(span * share, kv_local * head_size)
        out = []
        for g in range(kv_local):
            top, total, mixed = carry[3 * g : 3 * g + 3]
            mine = slice(g * head_size, (g + 1) * head_size)
            sc = lax.dot_general(queries[g], keys[:, mine], contract, preferred_element_type=F32)
            sc = sc / head_size
            higher = jnp.maximum(top, jnp.max(sc, axis=1, keepdims=True))
            shrink = jnp.exp(top - higher)
            weights = jnp.exp(sc - higher)
            total = total * shrink + jnp.sum(weights, axis=1, keepdims=True)
            mixed = mixed * shrink + jnp.dot(
                weights.astype(BF16), values[:, mine], preferred_element_type=F32
            )
            out += [higher, total, mixed]
        return tuple(out)

    if n == span:
        states = prefix(0, tuple(states))
    else:
        states = lax.fori_loop(0, n // span, lambda c, s: prefix(c * span, s), tuple(states))
    done = []
    for g in range(kv_local):
        _, total, mixed = states[3 * g : 3 * g + 3]
        result = mixed / total
        done += [result[j * block : (j + 1) * block] for j in range(group)]
    attended[...] = jnp.concatenate(done, axis=1).astype(BF16)

    def unpack(slot):
        t = gates_in[slot]
        gate_all[slot, 0:8] = t
        for i in range(1, rows // 8):
            gate_all[slot, 8 * i : 8 * i + 8] = pltpu.roll(t, 128 - 32 * i, 1)

    each(0, n, unpack)


def attend(n, hidden, key_own, value_own, docs, gates, rows, w_query, key_weight, value_weight):
    vmem = pl.BlockSpec(memory_space=pltpu.VMEM)
    hbm = pl.BlockSpec(memory_space=pltpu.HBM)
    return pl.pallas_call(
        functools.partial(attend_kernel, n),
        out_shape=(
            jax.ShapeDtypeStruct((hidden.shape[0], w_query.shape[1]), BF16),
            jax.ShapeDtypeStruct((n, rows, 128), F32),
        ),
        in_specs=[vmem] * 5 + [hbm] * 3,
        out_specs=(vmem, vmem),
        scratch_shapes=[
            pltpu.VMEM(w_query.shape, BF16),
            pltpu.VMEM(key_weight.shape, BF16),
            pltpu.VMEM(value_weight.shape, BF16),
            pltpu.VMEM((8, 128), F32),
            pltpu.VMEM((n,) + key_own.shape, BF16),
            pltpu.VMEM((n,) + value_own.shape, BF16),
            pltpu.VMEM((n, 8, 128), F32),
            pltpu.SemaphoreType.DMA((3,)),
            pltpu.SemaphoreType.DMA((3, n)),
            pltpu.SemaphoreType.DMA((3, n)),
        ],
        compiler_params=pltpu.CompilerParams(
            collective_id=0, has_side_effects=True, vmem_limit_bytes=60 << 20
        ),
    )(hidden, key_own, value_own, docs, gates, w_query, key_weight, value_weight)


def tail_kernel(
    n, n_tp, hparts,
    attended, hidden, gate_all, w_out_hbm, in_hbm, out_hbm,
    proj_ref, mix_ref, layer_ref,
    w_out, w_in, w_back, sums, outbox, inbox, tok, part, acc, cross, cross_in, home, home_in,
    o_sem, w_sem, tp_send, tp_recv, tok_send, tok_recv, x_send, x_recv, h_send, h_recv,
):
    half, ahead, behind = peers(n)
    units, ff = out_hbm.shape[0], out_hbm.shape[1]
    rows, width = proj_ref.shape
    me_tp = lax.axis_index("tp")
    chunk = min(4, half)

    def fetch(u):
        return (
            pltpu.make_async_copy(in_hbm.at[u], w_in.at[u], w_sem.at[0, u]),
            pltpu.make_async_copy(out_hbm.at[u], w_back.at[u], w_sem.at[1, u]),
        )

    out_fetch = pltpu.make_async_copy(w_out_hbm, w_out, o_sem)
    out_fetch.start()
    barrier = pltpu.get_barrier_semaphore()

    def greet(where):
        pl.semaphore_signal(barrier, inc=1, device_id=where, device_id_type=MESH)

    def tp_peer(t):
        return lax.rem(me_tp + t, n_tp)

    each(1, n_tp, lambda t: greet({"tp": tp_peer(t)}))
    each(1, half, lambda d: greet(ahead(0, d)))
    greet(ahead(1, 0))
    for u in range(units):
        for c in fetch(u):
            c.start()
    out_fetch.wait()
    whole = jnp.dot(attended[...], w_out[...], preferred_element_type=F32)
    sums[...] = whole
    outbox[...] = whole.astype(BF16)
    pl.semaphore_wait(barrier, n_tp - 1 + half)

    def tp_copy(t):
        return pltpu.make_async_remote_copy(
            src_ref=outbox.at[pl.ds(pl.multiple_of(tp_peer(t) * rows, rows), rows)],
            dst_ref=inbox.at[t],
            send_sem=tp_send.at[t],
            recv_sem=tp_recv.at[t],
            device_id={"tp": tp_peer(t)},
            device_id_type=MESH,
        )

    each(1, n_tp, lambda t: tp_copy(t).start())
    mine = pl.ds(pl.multiple_of(me_tp * rows, rows), rows)
    attn_sum = sums[mine, :]
    for t in range(1, n_tp):
        tp_copy(t).wait_recv()
        attn_sum = attn_sum + inbox[t].astype(F32)
    residual = hidden[mine, :].astype(F32) + RESIDUAL * attn_sum
    proj_ref[...] = attn_sum.astype(BF16)
    tok[0, 0] = normalize(residual).astype(BF16)

    def tok_copy(d):
        return pltpu.make_async_remote_copy(
            src_ref=tok.at[0, 0],
            dst_ref=tok.at[0, d],
            send_sem=tok_send.at[0, d],
            recv_sem=tok_recv.at[0, d],
            device_id=ahead(0, d),
            device_id_type=MESH,
        )

    def tok_cross(d):
        return pltpu.make_async_remote_copy(
            src_ref=tok.at[0, d],
            dst_ref=tok.at[1, d],
            send_sem=tok_send.at[1, d],
            recv_sem=tok_recv.at[1, d],
            device_id=ahead(1, 0),
            device_id_type=MESH,
        )

    def relay(d):
        tok_copy(d).wait_recv()
        tok_cross(d).start()

    each(1, half, lambda d: tok_copy(d).start())
    tok_cross(0).start()
    for u in range(units):
        for c in fetch(u):
            c.wait()
    each(1, half, relay)

    first_unit = lax.axis_index("seq") * units

    def experts(side, begin):
        tokens = tok[side, pl.ds(begin, chunk)].reshape(chunk * rows, width)
        gates = gate_all[pl.ds(side * half + begin, chunk)].reshape(chunk * rows, gate_all.shape[-1])
        lanes = lax.broadcasted_iota(jnp.int32, gates.shape, 1)
        acc[...] = jnp.zeros(acc.shape, F32)

        @pl.loop(0, units)
        def _(u):
            expert = (first_unit + u) // hparts
            weight = jnp.sum(jnp.where(lanes == expert, gates, 0.0), axis=1, keepdims=True)
            gate_up = jnp.dot(tokens, w_in[u], preferred_element_type=F32)
            active = (jax.nn.silu(gate_up[:, :ff]) * gate_up[:, ff:]).astype(BF16)
            back = jnp.dot(active, w_back[u], preferred_element_type=F32).astype(BF16)
            acc[...] += weight * back.astype(F32)

        total = acc[...].reshape(chunk, rows, width)
        if side == 0:
            part[pl.ds(begin, chunk)] = total
        else:
            cross[pl.ds(begin, chunk)] = total.astype(BF16)

    each(0, half // chunk, lambda c: experts(0, c * chunk))

    def cross_copy(d):
        return pltpu.make_async_remote_copy(
            src_ref=cross.at[d],
            dst_ref=cross_in.at[d],
            send_sem=x_send.at[d],
            recv_sem=x_recv.at[d],
            device_id=ahead(1, 0),
            device_id_type=MESH,
        )

    def send_cross(d):
        cross_copy(d).start()

    each(0, half, lambda d: tok_cross(d).wait_recv())
    each(0, half // chunk, lambda c: experts(1, c * chunk))
    each(1, half, send_cross)
    send_cross(0)

    def home_copy(d):
        return pltpu.make_async_remote_copy(
            src_ref=home.at[d],
            dst_ref=home_in.at[d],
            send_sem=h_send.at[d],
            recv_sem=h_recv.at[d],
            device_id=behind(0, d),
            device_id_type=MESH,
        )

    def send_home(d):
        cross_copy(d).wait_recv()
        home[d] = (part[d] + cross_in[d].astype(F32)).astype(BF16)
        home_copy(d).start()

    each(1, half, send_home)
    cross_copy(0).wait_recv()
    part[0] += cross_in[0].astype(F32)

    def collect(d):
        home_copy(d).wait_recv()
        part[0] += home_in[d].astype(F32)

    each(1, half, collect)
    expert_sum = part[0]
    mix_ref[...] = expert_sum.astype(BF16)
    layer_ref[...] = (residual + RESIDUAL * expert_sum).astype(BF16)

    each(1, n_tp, lambda t: tp_copy(t).wait_send())
    each(1, half, lambda d: tok_copy(d).wait_send())
    each(0, half, lambda d: tok_cross(d).wait_send())
    each(0, half, lambda d: cross_copy(d).wait_send())
    each(1, half, lambda d: home_copy(d).wait_send())


def tail(n, n_tp, attended, w_out, hidden, gate_all, expert_in, expert_out):
    half = n // 2
    block, width = hidden.shape
    rows = block // n_tp
    units, ff = expert_out.shape[:2]
    hparts = units * n // EXPERTS
    vmem = pl.BlockSpec(memory_space=pltpu.VMEM)
    hbm = pl.BlockSpec(memory_space=pltpu.HBM)
    out = jax.ShapeDtypeStruct((rows, width), BF16)
    dma = pltpu.SemaphoreType.DMA
    return pl.pallas_call(
        functools.partial(tail_kernel, n, n_tp, hparts),
        out_shape=(out, out, out),
        in_specs=[vmem, vmem, vmem, hbm, hbm, hbm],
        out_specs=(vmem, vmem, vmem),
        scratch_shapes=[
            pltpu.VMEM(w_out.shape, BF16),
            pltpu.VMEM(expert_in.shape, BF16),
            pltpu.VMEM(expert_out.shape, BF16),
            pltpu.VMEM((block, width), F32),
            pltpu.VMEM((block, width), BF16),
            pltpu.VMEM((n_tp, rows, width), BF16),
            pltpu.VMEM((2, half, rows, width), BF16),
            pltpu.VMEM((half, rows, width), F32),
            pltpu.VMEM((min(4, half) * rows, width), F32),
            pltpu.VMEM((half, rows, width), BF16),
            pltpu.VMEM((half, rows, width), BF16),
            pltpu.VMEM((half, rows, width), BF16),
            pltpu.VMEM((half, rows, width), BF16),
            dma,
            dma((2, units)),
            dma((n_tp,)),
            dma((n_tp,)),
            dma((2, half)),
            dma((2, half)),
            dma((half,)),
            dma((half,)),
            dma((half,)),
            dma((half,)),
        ],
        compiler_params=pltpu.CompilerParams(
            collective_id=1,
            has_side_effects=True,
            vmem_limit_bytes=62 << 20,
        ),
    )(attended, hidden, gate_all, w_out, expert_in, expert_out)


def body(
    hidden_in,
    w_query,
    key_weight,
    value_weight,
    w_out,
    cached_prefix_keys,
    cached_prefix_values,
    doc_ids,
    routes,
    gate_scores,
    expert_in,
    expert_out,
):
    n, n_tp = lax.axis_size("seq"), lax.axis_size("tp")
    experts = jnp.arange(128, dtype=jnp.int32)
    picked = routes.T[:, None, :] == experts[None, :, None]
    gates = jnp.sum(jnp.where(picked, gate_scores.T[:, None, :], 0.0), axis=0)
    gates = jnp.pad(gates, ((0, 0), (0, 128 - routes.shape[0])))
    attended, gate_all = attend(
        n, hidden_in, cached_prefix_keys, cached_prefix_values, doc_ids, gates, routes.shape[0],
        w_query, key_weight, value_weight,
    )
    return tail(n, n_tp, attended, w_out, hidden_in, gate_all, expert_in, expert_out)


def solution(mesh):
    in_specs = (
        P("seq", None),
        P(None, "tp"),
        P(None, "tp"),
        P(None, "tp"),
        P("tp", None),
        P("seq", "tp"),
        P("seq", "tp"),
        P("seq", None),
        P(("seq", "tp"), None),
        P(("seq", "tp"), None),
        P("seq", None, None),
        P("seq", None, None),
    )
    out_specs = (P(("seq", "tp"), None), P(("seq", "tp"), None), P(("seq", "tp"), None))
    return jax.shard_map(body, mesh=mesh, in_specs=in_specs, out_specs=out_specs, check_vma=False)
```
